32 devices in a mesh: lat: 8 (over z, y), lon: 4 (over x, core).
Axes of the slice: x: 2, y: 2, z: 4, core: 2. Of those that a mesh axis runs over, the one named last changes fastest.
Arguments:
- cube_cells: bfloat16 [1536, 80, 128], P(('lat', 'lon')), may hold values from -6 to 6
- block_source: int32 [720, 4, 4], P('lat', 'lon'), may hold values from 0 to 191, as said below
- block_weight: bfloat16 [720, 4, 4, 360, 128], P('lat', 'lon'), may hold values from -0.25 to 0.25
- lift_in: bfloat16 [80, 256], replicated, may hold values from -0.625 to 0.625
- lift_out: bfloat16 [256, 256], replicated, may hold values from -0.375 to 0.375
- spectral: bfloat16 [384, 256, 256], P('lon'), may hold values from -1.5 to 1.5
Outputs:
- grid_field: bfloat16 [720, 1440, 256], P('lat', 'lon')
The draws below stay inside these ranges and needn't reach their ends.
Inputs may be any that keep to these rules, and one draw needn't show every extreme that they name: `block_source`: for target row r in band i = r // 90 and longitude block J, every entry is a position among band i's 192 tiles lying cyclically within 24 positions below or above the positions J * 48 to (J + 1) * 48 - 1. In the first row of every band and block, the first entry is the lowest position of that range and the second the highest.
All inputs are finite; a program needn't handle non-finite values.
Results may differ from the reference program's by a relative error of at most 0.015.
Values may be sent and summed in bfloat16 or wider, within the bound.
A program may use at most 320 MiB of HBM per device.

```python
import math
import jax
import jax.numpy as jnp
from jax import lax

CIN = 80
C = 256
NLAT = 720
NLON = 1440
L = 384
TILE = 128
K = 4
SRC_DEV = 48
RIM = 24
LAT_DEV = 90
LON_DEV = 360
BAND_TILES = 192
SRC_TILES = 1536
N_LAT = 8
N_LON = 4


def draw_block_source(key, part):
    key = jax.random.fold_in(key, 7)
    window_size = SRC_DEV + 2 * RIM
    position = jax.random.randint(key, (NLAT, N_LON, K), 0, window_size, dtype=jnp.int32)
    row_index = jnp.arange(NLAT, dtype=jnp.int32)[:, None, None]
    slot_index = jnp.arange(K, dtype=jnp.int32)[None, None, :]
    leading = row_index % LAT_DEV == 0
    position = jnp.where(leading & (slot_index == 0), 0, position)
    position = jnp.where(leading & (slot_index == 1), window_size - 1, position)
    lon_block = jnp.arange(N_LON, dtype=jnp.int32)[None, :, None]
    return ((lon_block * SRC_DEV - RIM + position) % BAND_TILES).astype(jnp.int32)


def shard_levels(rng, shape, split, smallest, high):
    loudness, own = 1.0, jax.random.fold_in(rng, 6)
    for dim, parts in split:
        steps = jnp.exp(jax.random.uniform(jax.random.fold_in(own, dim), (parts,), jnp.float32, smallest / len(split), high / len(split)))
        loudness = loudness * jnp.repeat(steps, shape[dim] // parts).reshape([-1 if axis == dim else 1 for axis in range(len(shape))])
    return loudness


def noise(rng, extent, spread, most, cuts=(), kind=jnp.bfloat16):
    loudness = shard_levels(rng, extent, cuts, -0.22, 0.18) if cuts else 1.0
    entries = jax.random.normal(rng, extent, jnp.float32) * spread * loudness
    return jnp.minimum(jnp.maximum(entries, -most), most).astype(kind)


def setup_inputs(seed: int = 0) -> dict:
    seeds = jax.random.split(jax.random.key(seed), 7)
    cube_cells = noise(seeds[0], (SRC_TILES, CIN, TILE), 1.0, 6.0, ((0, 32),))
    block_source = draw_block_source(jax.random.fold_in(seeds[6], 71), 0)
    block_weight = noise(seeds[2], (NLAT, N_LON, K, LON_DEV, TILE), (K * TILE) ** -0.5, 0.25, ((0, 8), (1, 4)))
    lift_in = noise(seeds[3], (CIN, C), CIN ** -0.5, 0.625)
    lift_out = noise(seeds[4], (C, C), C ** -0.5, 0.375)
    spectral = noise(seeds[5], (L, C, C), (C // 16) ** -0.5, 1.5, ((0, 4),))
    return dict(cube_cells=cube_cells, block_source=block_source, block_weight=block_weight, lift_in=lift_in, lift_out=lift_out, spectral=spectral)


def legendre_setup(wave_orders):
    colatitude = (jnp.arange(NLAT, dtype=jnp.float32) + 0.5) * (math.pi / NLAT)
    cosine = jnp.cos(colatitude)[None, :]
    order_col = wave_orders.astype(jnp.float32)[:, None]
    log_scale = 0.5 * (jnp.log(2.0 * order_col + 1.0) - math.log(4.0 * math.pi) + lax.lgamma(2.0 * order_col + 1.0) - 2.0 * lax.lgamma(order_col + 1.0) - order_col * math.log(4.0)) + order_col * jnp.log(jnp.sin(colatitude))[None, :]
    initial = jnp.exp(jnp.minimum(log_scale + 80.0, 0.0))
    restore = jnp.exp(jnp.maximum(log_scale, -80.0))
    quadrature = jnp.sin(colatitude) * (math.pi / NLAT) * (2.0 * math.pi / NLON)
    return (cosine, order_col, initial, restore, quadrature)

def legendre_step(degree, current, earlier, cosine, order_col, initial):
    square = degree * degree
    rising = jnp.sqrt(jnp.maximum(4.0 * square - 1.0, 1.0) / jnp.maximum(square - order_col * order_col, 1.0))
    shifted = (degree - 1.0) * (degree - 1.0)
    falling = jnp.sqrt(jnp.maximum(shifted - order_col * order_col, 0.0) / jnp.maximum(4.0 * shifted - 1.0, 1.0))
    advanced = rising * (cosine * current - falling * earlier)
    return jnp.where(degree < order_col, 0.0, jnp.where(degree == order_col, initial, advanced))

def legendre_tables(wave_orders):
    cosine, order_col, initial, restore, quadrature = legendre_setup(wave_orders)

    def advance(carry, degree_index):
        current, earlier = carry
        latest = legendre_step(degree_index.astype(jnp.float32), current, earlier, cosine, order_col, initial)
        return ((latest, current), latest * restore)
    zeroed = jnp.zeros((wave_orders.shape[0], NLAT), jnp.float32)
    _, table = lax.scan(advance, (zeroed, zeroed), jnp.arange(L, dtype=jnp.int32))
    return ((table * quadrature[None, None, :]).astype(jnp.bfloat16), table.astype(jnp.bfloat16))

def fourier_table(wave_orders):
    longitude = jnp.arange(NLON, dtype=jnp.int32)
    phase = longitude[:, None] * wave_orders[None, :] % NLON
    angle = phase.astype(jnp.float32) * (2.0 * math.pi / NLON)
    paired = jnp.stack([jnp.cos(angle), -jnp.sin(angle)], axis=2)
    return paired.reshape(NLON, 2 * wave_orders.shape[0])

def reference(cube_cells, block_source, block_weight, lift_in, lift_out, spectral):
    lat_dev = NLAT // N_LAT
    lon_dev = NLON // N_LON
    block_width = min(128, L)
    band_cells = cube_cells.reshape(N_LAT, N_LON * SRC_DEV, CIN, TILE)
    band_sources = block_source.reshape(N_LAT, lat_dev, N_LON, K)
    band_weights = block_weight.reshape(N_LAT, lat_dev, N_LON, K, lon_dev, TILE)
    all_orders = jnp.arange(L, dtype=jnp.int32)
    table_wide = fourier_table(all_orders)
    forward = table_wide.astype(jnp.bfloat16)
    factors = jnp.repeat(jnp.where(all_orders == 0, 1.0, 2.0), 2)
    inverse = (table_wide * factors[None, :]).astype(jnp.bfloat16)
    lift_first = lift_in.astype(jnp.float32)
    lift_second = lift_out.astype(jnp.float32)
    forward_wide = forward.astype(jnp.float32)
    inverse_wide = inverse.astype(jnp.float32)
    spectral_wide = spectral.astype(jnp.float32)

    def band_spectrum(inputs):
        tiles_band, source_band, weight_band = inputs
        picked = tiles_band[source_band]
        remapped = jnp.einsum('rjkts,rjkcs->rjtc', weight_band.astype(jnp.float32), picked.astype(jnp.float32)).astype(jnp.bfloat16)
        remapped = remapped.reshape(lat_dev, NLON, CIN)
        hidden = jax.nn.gelu(jnp.einsum('rtc,cd->rtd', remapped.astype(jnp.float32), lift_first)).astype(jnp.bfloat16)
        lifted = jnp.einsum('rtd,de->rte', hidden.astype(jnp.float32), lift_second).astype(jnp.bfloat16)
        return jnp.einsum('rte,tq->req', lifted.astype(jnp.float32), forward_wide).astype(jnp.bfloat16)
    spectra = lax.map(band_spectrum, (band_cells, band_sources, band_weights)).reshape(NLAT, C, L, 2)

    def group_synthesis(group_start):
        group_orders = group_start + jnp.arange(block_width, dtype=jnp.int32)
        weighted, plain = legendre_tables(group_orders)
        section = lax.dynamic_slice_in_dim(spectra, group_start, block_width, 2)
        analysis = jnp.einsum('lmt,tcmp->mcpl', weighted.astype(jnp.float32), section.astype(jnp.float32)).astype(jnp.bfloat16)
        mixed_modes = jnp.einsum('mcpl,lcd->mlpd', analysis.astype(jnp.float32), spectral_wide).astype(jnp.bfloat16)
        return jnp.einsum('lmt,mlpd->mpdt', plain.astype(jnp.float32), mixed_modes.astype(jnp.float32)).astype(jnp.bfloat16)
    synthesis = lax.map(group_synthesis, jnp.arange(0, L, block_width, dtype=jnp.int32)).reshape(2 * L, C, NLAT)

    def band_grid(band_number):
        rows_band = lax.dynamic_slice_in_dim(synthesis, band_number * lat_dev, lat_dev, 2)
        return jnp.einsum('qct,kq->tkc', rows_band.astype(jnp.float32), inverse_wide).astype(jnp.bfloat16)
    grid_field = lax.map(band_grid, jnp.arange(N_LAT, dtype=jnp.int32)).reshape(NLAT, NLON, C)
    return grid_field
```

```python
import math

import jax
import jax.numpy as jnp
from jax import lax
from jax.experimental import pallas as pl
from jax.experimental.pallas import tpu as pltpu
from jax.sharding import PartitionSpec as P

NLAT = 720
NLON = 1440
L = 384
SRC_DEV = 48


unroll_steps = 16


def extended(cells, sides, width):
    for axis, dim in sides:
        count = lax.axis_size(axis)
        head = lax.slice_in_dim(cells, 0, width, axis=dim)
        tail = lax.slice_in_dim(cells, cells.shape[dim] - width, cells.shape[dim], axis=dim)
        cells = jnp.concatenate(
            [
                lax.ppermute(tail, axis, [(i, (i + 1) % count) for i in range(count)]),
                cells,
                lax.ppermute(head, axis, [((i + 1) % count, i) for i in range(count)]),
            ],
            axis=dim,
        )
    return cells


def legendre_setup(wave_orders):
    colatitude = (jnp.arange(NLAT, dtype=jnp.float32) + 0.5) * (math.pi / NLAT)
    cosine = jnp.cos(colatitude)[None, :]
    order_col = wave_orders.astype(jnp.float32)[:, None]
    log_scale = (
        0.5
        * (
            jnp.log(2.0 * order_col + 1.0)
            - math.log(4.0 * math.pi)
            + lax.lgamma(2.0 * order_col + 1.0)
            - 2.0 * lax.lgamma(order_col + 1.0)
            - order_col * math.log(4.0)
        )
        + order_col * jnp.log(jnp.sin(colatitude))[None, :]
    )
    initial = jnp.exp(jnp.minimum(log_scale + 80.0, 0.0))
    restore = jnp.exp(jnp.maximum(log_scale, -80.0))
    quadrature = jnp.sin(colatitude) * (math.pi / NLAT) * (2.0 * math.pi / NLON)
    return (cosine, order_col, initial, restore, quadrature)


def legendre_step(degree, current, earlier, cosine, order_col, initial):
    square = degree * degree
    rising = jnp.sqrt(
        jnp.maximum(4.0 * square - 1.0, 1.0) / jnp.maximum(square - order_col * order_col, 1.0)
    )
    shifted = (degree - 1.0) * (degree - 1.0)
    falling = jnp.sqrt(
        jnp.maximum(shifted - order_col * order_col, 0.0) / jnp.maximum(4.0 * shifted - 1.0, 1.0)
    )
    advanced = rising * (cosine * current - falling * earlier)
    return jnp.where(degree < order_col, 0.0, jnp.where(degree == order_col, initial, advanced))


def legendre_tables(wave_orders):
    cosine, order_col, initial, restore, quadrature = legendre_setup(wave_orders)

    def advance(carry, base_degree):
        current, earlier = carry
        stacked = []
        for offset in range(unroll_steps):
            latest = legendre_step(
                (base_degree + offset).astype(jnp.float32),
                current,
                earlier,
                cosine,
                order_col,
                initial,
            )
            earlier = current
            current = latest
            stacked.append(latest * restore)
        return ((current, earlier), jnp.stack(stacked))

    zeroed = jnp.zeros((wave_orders.shape[0], NLAT), jnp.float32)
    _, pieces = lax.scan(advance, (zeroed, zeroed), jnp.arange(0, L, unroll_steps, dtype=jnp.int32))
    table = pieces.reshape(L, wave_orders.shape[0], NLAT)
    return ((table * quadrature[None, None, :]).astype(jnp.bfloat16), table.astype(jnp.bfloat16))


def fourier_table(wave_orders):
    longitude = jnp.arange(NLON, dtype=jnp.int32)
    phase = longitude[:, None] * wave_orders[None, :] % NLON
    angle = phase.astype(jnp.float32) * (2.0 * math.pi / NLON)
    paired = jnp.stack([jnp.cos(angle), -jnp.sin(angle)], axis=2)
    return paired.reshape(NLON, 2 * wave_orders.shape[0])


def to_bands(values):
    return lax.all_to_all(values, "lat", split_axis=2, concat_axis=0, tiled=True)


def regroup(values):
    return lax.all_to_all(values, "lon", split_axis=3, concat_axis=1, tiled=True)


def analyse(table_part, data_part, first_block, block_width):
    order_count = table_part.shape[1]
    channel_count = data_part.shape[1]

    def fill_block(block_index, accumulated):
        table_block = lax.dynamic_slice_in_dim(
            table_part, block_index * block_width, block_width, 0
        )
        partial_value = jnp.einsum(
            "lmt,tcmp->mcpl", table_block, data_part, preferred_element_type=jnp.float32
        )
        return lax.dynamic_update_slice_in_dim(
            accumulated, partial_value, block_index * block_width, 3
        )

    zeroed = jnp.zeros((order_count, channel_count, 2, L), jnp.float32)
    return lax.fori_loop(first_block, L // block_width, fill_block, zeroed)


def synthesise(table_part, data_part, first_block, block_width):
    order_count = table_part.shape[1]
    channel_count = data_part.shape[3]

    def add_block(block_index, accumulated):
        table_block = lax.dynamic_slice_in_dim(
            table_part, block_index * block_width, block_width, 0
        )
        degree_rows = lax.dynamic_slice_in_dim(data_part, block_index * block_width, block_width, 1)
        return accumulated + jnp.einsum(
            "lmt,mlpd->mpdt", table_block, degree_rows, preferred_element_type=jnp.float32
        )

    zeroed = jnp.zeros((order_count, 2, channel_count, NLAT), jnp.float32)
    return lax.fori_loop(first_block, L // block_width, add_block, zeroed)


def shards(cube_cells, block_source, block_weight, lift_in, lift_out, spectral):
    lat_count = lax.axis_size("lat")
    lon_count = lax.axis_size("lon")
    lat_index = lax.axis_index("lat")
    lon_index = lax.axis_index("lon")
    block_width = min(128, L)
    rim_tiles = SRC_DEV // 2
    per_band = L // lat_count
    half_size = per_band // 2
    slot_index = jnp.arange(per_band, dtype=jnp.int32)[None, :]
    band_index = jnp.arange(lat_count, dtype=jnp.int32)[:, None]
    all_orders = band_index * per_band + slot_index
    column_orders = all_orders.reshape(lat_count * per_band)
    own_orders = lax.dynamic_index_in_dim(all_orders, lat_index, 0, keepdims=False)
    table_wide = fourier_table(column_orders)
    forward = table_wide.astype(jnp.bfloat16)
    widened = extended(cube_cells, (("lon", 0),), rim_tiles)
    band_tiles = lon_count * SRC_DEV
    offsets = (block_source[:, 0, :] - lon_index * SRC_DEV + rim_tiles) % band_tiles
    picked = widened[offsets]
    remapped = jnp.einsum(
        "rkts,rkcs->rtc", block_weight[:, 0], picked, preferred_element_type=jnp.float32
    ).astype(jnp.bfloat16)
    hidden = jax.nn.gelu(
        jnp.einsum("rtc,cd->rtd", remapped, lift_in, preferred_element_type=jnp.float32)
    ).astype(jnp.bfloat16)
    lifted = jnp.einsum("rtd,de->ret", hidden, lift_out, preferred_element_type=jnp.float32).astype(
        jnp.bfloat16
    )
    grid_rows = lax.all_to_all(lifted, "lon", split_axis=1, concat_axis=2, tiled=True)
    spectra = jnp.einsum(
        "rcl,lq->rcq", grid_rows, forward, preferred_element_type=jnp.float32
    ).astype(jnp.bfloat16)
    gathered = to_bands(spectra)
    channel_count = gathered.shape[1]
    gathered = gathered.reshape(NLAT, channel_count, per_band, 2)
    weighted, plain_table = legendre_tables(own_orders)
    sections = []
    for half_index in range(2):
        lowest = half_index * half_size
        first_block = own_orders[lowest] // block_width
        sections.append(
            analyse(
                weighted[:, lowest : lowest + half_size, :],
                gathered[:, :, lowest : lowest + half_size, :],
                first_block,
                block_width,
            )
        )
    analysis = jnp.concatenate(sections, axis=0).astype(jnp.bfloat16)
    by_degree = regroup(analysis)
    mixed_modes = jnp.einsum(
        "mcpl,lcd->mlpd", by_degree, spectral, preferred_element_type=jnp.float32
    ).astype(jnp.bfloat16)
    returned = regroup(mixed_modes)
    pieces = []
    for half_index in range(2):
        lowest = half_index * half_size
        first_block = own_orders[lowest] // block_width
        pieces.append(
            synthesise(
                plain_table[:, lowest : lowest + half_size, :],
                returned[lowest : lowest + half_size],
                first_block,
                block_width,
            )
        )
    synthesized = (
        jnp.concatenate(pieces, axis=0)
        .astype(jnp.bfloat16)
        .reshape(2 * per_band, channel_count, NLAT)
    )
    rows_back = to_bands(synthesized)
    factors = jnp.repeat(jnp.where(column_orders == 0, 1.0, 2.0), 2).astype(jnp.bfloat16)
    inverse = forward * factors[None, :]
    grid_field = jnp.einsum(
        "qcr,kq->rkc", rows_back, inverse, preferred_element_type=jnp.float32
    ).astype(jnp.bfloat16)
    return lax.all_to_all(grid_field, "lon", split_axis=1, concat_axis=2, tiled=True)


PARTS = 3
PAIRS = 3
STEP = 16
F32 = jnp.float32
BF16 = jnp.bfloat16


def params():
    return pltpu.CompilerParams(vmem_limit_bytes=56 * 1024 * 1024)


def cost(flops, moved):
    return pl.CostEstimate(flops=flops, bytes_accessed=moved, transcendentals=0)


def whole_block(shape):
    zeros = (0,) * len(shape)
    return pl.BlockSpec(shape, lambda *_: zeros)


def halves(left, right, at):
    return jnp.concatenate([left[:, at : at + 64], right[:, at : at + 64]], axis=1)


def lift_kernel(first_row, picks, tiles, weight, lift_in, lift_out, out):
    rows = []
    for r in range(2):
        row = first_row + pl.program_id(0) * 2 + r
        source = jnp.concatenate([tiles[picks[row * 4 + k]] for k in range(4)], axis=1)
        blocks = jnp.concatenate([weight[r, k] for k in range(4)], axis=1)
        remapped = lax.dot_general(
            blocks, source, (((1,), (1,)), ((), ())), preferred_element_type=F32
        ).astype(BF16)
        hidden = jax.nn.gelu(jnp.dot(remapped, lift_in[...], preferred_element_type=F32))
        rows.append(
            jnp.dot(hidden.astype(BF16), lift_out[...], preferred_element_type=F32).astype(BF16)
        )
    for q in range(4):
        out[q, 0] = halves(rows[0], rows[1], 64 * q)


def lift_part(part, pairs, picks, tiles, weight, lift_in, lift_out):
    width = weight.shape[2]
    return pl.pallas_call(
        lambda *refs: lift_kernel(part * pairs * 2, *refs),
        out_shape=jax.ShapeDtypeStruct((4, pairs, width, 128), BF16),
        grid_spec=pltpu.PrefetchScalarGridSpec(
            num_scalar_prefetch=1,
            grid=(pairs,),
            in_specs=[
                whole_block(tiles.shape),
                pl.BlockSpec((2, 4, width, 128), lambda g, _: (part * pairs + g, 0, 0, 0)),
                whole_block(lift_in.shape),
                whole_block(lift_out.shape),
            ],
            out_specs=pl.BlockSpec((4, 1, width, 128), lambda g, _: (0, g, 0, 0)),
        ),
        compiler_params=params(),
        cost_estimate=cost(pairs * 2 * width * 256 * 256 * 4, pairs * width * 128 * 24),
        name="lift_rows",
    )(picks, tiles, weight, lift_in, lift_out)


def dft_kernel(table, data, scale, out):
    total = None
    for j in range(4):
        block = jnp.concatenate([data[j, g] for g in range(PAIRS)], axis=1)
        term = jnp.dot(table[j], block, preferred_element_type=F32)
        total = term if total is None else total + term
    total = total * scale[0]
    half = total.shape[0] // 2
    orders = half // 8
    for r in range(2 * PAIRS):
        row = halves(total[:half], total[half:], 64 * r).astype(BF16)
        for i in range(8):
            out[i, r] = row[i * orders : (i + 1) * orders]


def dft_part(table, data, scale):
    _, pairs, width, _ = data.shape
    waves = table.shape[1]
    rows = 2 * PAIRS
    return pl.pallas_call(
        dft_kernel,
        out_shape=jax.ShapeDtypeStruct((8, 2 * pairs, waves // 16, 128), BF16),
        grid=(pairs // PAIRS,),
        in_specs=[
            whole_block(table.shape),
            pl.BlockSpec((4, PAIRS, width, 128), lambda g: (0, g, 0, 0)),
            pl.BlockSpec((1, 1, 64 * rows), lambda g: (g, 0, 0)),
        ],
        out_specs=pl.BlockSpec((8, rows, waves // 16, 128), lambda g: (0, g, 0, 0)),
        compiler_params=params(),
        cost_estimate=cost(pairs * 128 * 4 * width * waves * 2, pairs * 128 * 4 * width * 4),
        name="forward_rows",
    )(table, data, scale)


def legendre_kernel(cosine, order, initial, restore, out, current, earlier, held):
    base = pl.program_id(0) * STEP

    @pl.when(base == 0)
    def _():
        current[...] = jnp.zeros_like(current)
        earlier[...] = jnp.zeros_like(earlier)

    orders = order.shape[0]
    now, before = current[...], earlier[...]
    for s in range(STEP):
        degree = (base + s).astype(F32)
        square = degree * degree
        order_square = order[...] * order[...]
        rising = jnp.sqrt(
            jnp.maximum(4.0 * square - 1.0, 1.0) / jnp.maximum(square - order_square, 1.0)
        )
        shifted = (degree - 1.0) * (degree - 1.0)
        falling = jnp.sqrt(
            jnp.maximum(shifted - order_square, 0.0) / jnp.maximum(4.0 * shifted - 1.0, 1.0)
        )
        advanced = rising * (cosine[...] * now - falling * before)
        latest = jnp.where(
            degree < order[...], 0.0, jnp.where(degree == order[...], initial[...], advanced)
        )
        now, before = latest, now
        held[s] = latest * restore[...]
    current[...] = now
    earlier[...] = before
    out[...] = jnp.swapaxes(held[...], 0, 1)[:, :, : out.shape[2]].astype(BF16)


def legendre_table(orders, row_order):
    cosine, order_col, initial, restore, quadrature = legendre_setup(orders)
    extra = ((0, 0), (0, -NLAT % 128))
    cosine, initial, restore = (
        jnp.pad(value[:, row_order], extra) for value in (cosine, initial, restore)
    )
    count, wide = initial.shape
    table = pl.pallas_call(
        legendre_kernel,
        out_shape=jax.ShapeDtypeStruct((count, L, NLAT), BF16),
        grid=(L // STEP,),
        in_specs=[
            whole_block((1, wide)),
            whole_block((count, 1)),
            whole_block((count, wide)),
            whole_block((count, wide)),
        ],
        out_specs=pl.BlockSpec((count, STEP, NLAT), lambda g: (0, g, 0)),
        scratch_shapes=[
            pltpu.VMEM((count, wide), F32),
            pltpu.VMEM((count, wide), F32),
            pltpu.VMEM((STEP, count, wide), F32),
        ],
        compiler_params=params(),
        cost_estimate=cost(L * count * wide * 100, count * L * NLAT * 2),
        name="legendre_table",
    )(cosine, order_col, initial, restore)
    return table, quadrature


def analysis_kernel(table, first, second, third, out):
    for m in range(table.shape[0]):
        rows = jnp.concatenate([first[m], second[m], third[m]], axis=0)
        out[m] = jnp.dot(table[m], rows, preferred_element_type=F32).astype(BF16)


def analysis_all(table, pieces, group=4):
    count = table.shape[0]
    depth = pieces[0].shape[1]
    return pl.pallas_call(
        analysis_kernel,
        out_shape=jax.ShapeDtypeStruct((count, L, 128), BF16),
        grid=(count // group,),
        in_specs=[pl.BlockSpec((group, L, NLAT), lambda g: (g, 0, 0))]
        + [pl.BlockSpec((group, depth, 128), lambda g: (g, 0, 0))] * 3,
        out_specs=pl.BlockSpec((group, L, 128), lambda g: (g, 0, 0)),
        compiler_params=params(),
        cost_estimate=cost(count * L * NLAT * 256, count * L * NLAT * 2),
        name="analysis",
    )(table, *pieces)


def mix_kernel(data, matrix, out):
    for l in range(data.shape[1]):
        sides = []
        for p in range(2):
            sides.append(
                jnp.concatenate([data[j, l][:, 64 * p : 64 * p + 64] for j in range(4)], axis=1)
            )
        joined = jnp.concatenate(sides, axis=0)
        mixed = jnp.dot(joined, matrix[l], preferred_element_type=F32).astype(BF16)
        count = data.shape[2]
        for q in range(4):
            out[q, l] = halves(mixed[:count], mixed[count:], 64 * q)


def mix_all(data, matrix, group=8):
    _, degrees, count, _ = data.shape
    spec = pl.BlockSpec((4, group, count, 128), lambda g: (0, g, 0, 0))
    return pl.pallas_call(
        mix_kernel,
        out_shape=jax.ShapeDtypeStruct(data.shape, BF16),
        grid=(degrees // group,),
        in_specs=[spec, pl.BlockSpec((group, 256, 256), lambda g: (g, 0, 0))],
        out_specs=spec,
        compiler_params=params(),
        cost_estimate=cost(degrees * count * 4 * 256 * 256, degrees * 256 * 256 * 2),
        name="mixing",
    )(data, matrix)


def synthesis_kernel(table, data, first, second, third):
    for m in range(table.shape[0]):
        value = lax.dot_general(
            table[m], data[m], (((0,), (0,)), ((), ())), preferred_element_type=F32
        ).astype(BF16)
        depth = first.shape[1]
        first[m] = value[:depth]
        second[m] = value[depth : 2 * depth]
        third[m] = value[2 * depth :]


def synthesis_all(table, data, group=4):
    count = table.shape[0]
    depth = NLAT // PARTS
    return pl.pallas_call(
        synthesis_kernel,
        out_shape=[jax.ShapeDtypeStruct((count, depth, 128), BF16)] * 3,
        grid=(count // group,),
        in_specs=[
            pl.BlockSpec((group, L, NLAT), lambda g: (g, 0, 0)),
            pl.BlockSpec((group, L, 128), lambda g: (g, 0, 0)),
        ],
        out_specs=[pl.BlockSpec((group, depth, 128), lambda g: (g, 0, 0))] * 3,
        compiler_params=params(),
        cost_estimate=cost(count * L * NLAT * 256, count * L * NLAT * 2),
        name="synthesis",
    )(table, data)


def inverse_kernel(table, data, out):
    columns = [[], []]
    for r in range(2 * PAIRS):
        row = jnp.concatenate([data[i, r] for i in range(8)], axis=0)
        for p in range(2):
            columns[p].append(row[:, 64 * p : 64 * p + 64])
    joined = jnp.concatenate([jnp.concatenate(side, axis=1) for side in columns], axis=0)
    for j in range(4):
        value = jnp.dot(table[j], joined, preferred_element_type=F32).astype(BF16)
        for g in range(PAIRS):
            out[j, g] = value[:, 128 * g : 128 * g + 128]


def inverse_part(table, data):
    _, rows, orders, _ = data.shape
    width = table.shape[1]
    return pl.pallas_call(
        inverse_kernel,
        out_shape=jax.ShapeDtypeStruct((4, rows // 2, width, 128), BF16),
        grid=(rows // (2 * PAIRS),),
        in_specs=[
            whole_block(table.shape),
            pl.BlockSpec((8, 2 * PAIRS, orders, 128), lambda g: (0, g, 0, 0)),
        ],
        out_specs=pl.BlockSpec((4, PAIRS, width, 128), lambda g: (0, g, 0, 0)),
        compiler_params=params(),
        cost_estimate=cost(rows * 64 * 4 * width * 16 * orders * 2, rows * 64 * 4 * width * 4),
        name="inverse_rows",
    )(table, data)


def join_kernel(data, prior, out):
    for r in range(2):
        out[r] = jnp.concatenate(
            [data[j, 0][:, 64 * r : 64 * r + 64] for j in range(4)], axis=1
        )


def join_part(part, data, prior):
    _, pairs, width, _ = data.shape
    rows = 2 * pairs * PARTS
    shape = jax.ShapeDtypeStruct((rows, width, 256), BF16)
    first = prior is None
    return pl.pallas_call(
        (lambda data, out: join_kernel(data, None, out)) if first else join_kernel,
        out_shape=shape,
        grid=(pairs,),
        in_specs=[pl.BlockSpec((4, 1, width, 128), lambda g: (0, g, 0, 0))]
        + ([] if first else [pl.BlockSpec(memory_space=pl.ANY)]),
        out_specs=pl.BlockSpec((2, width, 256), lambda g: (part * pairs + g, 0, 0)),
        input_output_aliases={} if first else {1: 0},
        compiler_params=params(),
        cost_estimate=cost(0, pairs * width * 256 * 8),
        name="join_rows",
    )(*((data,) if first else (data, prior)))


def swap(values, axis):
    return lax.all_to_all(values, axis, split_axis=0, concat_axis=0, tiled=True)


def fourier_pair(lon_count):
    orders = jnp.arange(L, dtype=jnp.int32)
    longitude = jnp.arange(NLON, dtype=jnp.int32).reshape(lon_count, 1, NLON // lon_count)
    phase = (longitude * orders[None, :, None]) % NLON
    angle = phase.astype(F32) * (2.0 * math.pi / NLON)
    forward = jnp.concatenate([jnp.cos(angle), -jnp.sin(angle)], axis=1).astype(BF16)
    factor = jnp.where(orders == 0, 1.0, 2.0).astype(BF16)
    inverse = forward * jnp.tile(factor, 2)[None, :, None]
    return forward, jnp.swapaxes(inverse, 1, 2)


def packed_shards(cube_cells, block_source, block_weight, lift_in, lift_out, spectral):
    lat_count = lax.axis_size("lat")
    lon_count = lax.axis_size("lon")
    lon_index = lax.axis_index("lon")
    rows = block_weight.shape[0]
    pairs = rows // (2 * PARTS)
    per_band = L // lat_count
    rim_tiles = SRC_DEV // 2
    own_orders = lax.axis_index("lat") * per_band + jnp.arange(per_band, dtype=jnp.int32)

    widened = extended(cube_cells, (("lon", 0),), rim_tiles)
    picks = (block_source[:, 0, :] - lon_index * SRC_DEV + rim_tiles) % (lon_count * SRC_DEV)
    picks = picks.reshape(-1)
    weight = block_weight[:, 0]
    forward, inverse = fourier_pair(lon_count)
    row_order = jnp.arange(NLAT, dtype=jnp.int32).reshape(lat_count, PARTS, 2 * pairs)
    row_order = jnp.swapaxes(row_order, 0, 1).reshape(NLAT)
    table, quadrature = legendre_table(own_orders, row_order)
    own_scale = lax.dynamic_slice_in_dim(quadrature, lax.axis_index("lat") * rows, rows)
    own_scale = jnp.repeat(own_scale, 64).reshape(PARTS, pairs // PAIRS, 1, 128 * PAIRS)

    pieces = []
    for part in range(PARTS):
        lifted = lift_part(part, pairs, picks, widened, weight, lift_in, lift_out)
        spectra = dft_part(forward, swap(lifted, "lon"), own_scale[part])
        gathered = swap(spectra, "lat").reshape(NLAT // PARTS, per_band, 128)
        pieces.append(jnp.swapaxes(gathered, 0, 1))
    analysis = analysis_all(table, pieces)
    split = analysis.reshape(per_band, lon_count, L // lon_count, 128)
    by_degree = swap(jnp.transpose(split, (1, 2, 0, 3)), "lon")
    returned = swap(mix_all(by_degree, spectral), "lon").reshape(L, per_band, 128)
    synthesized = synthesis_all(table, jnp.swapaxes(returned, 0, 1))
    grid_field = None
    for part in range(PARTS):
        sent = jnp.swapaxes(synthesized[part], 0, 1)
        sent = sent.reshape(lat_count, 2 * pairs, per_band, 128)
        placed = inverse_part(inverse, swap(sent, "lat"))
        grid_field = join_part(part, swap(placed, "lon"), grid_field)
    return grid_field


def solution(mesh):
    packed = mesh.shape["lat"] == 8 and mesh.shape["lon"] == 4
    in_specs = (
        P(("lat", "lon"), None, None),
        P("lat", "lon", None),
        P("lat", "lon", None, None, None),
        P(),
        P(),
        P("lon", None, None),
    )
    out_specs = P("lat", "lon", None)
    return jax.shard_map(packed_shards if packed else shards, mesh=mesh, in_specs=in_specs, out_specs=out_specs, check_vma=False)
```

```python
import math

import jax
import jax.numpy as jnp
from jax import lax
from jax.experimental import pallas as pl
from jax.experimental.pallas import tpu as pltpu
from jax.sharding import PartitionSpec as P

NLAT = 720
NLON = 1440
L = 384
SRC_DEV = 48


unroll_steps = 16


def extended(cells, sides, width):
    for axis, dim in sides:
        count = lax.axis_size(axis)
        head = lax.slice_in_dim(cells, 0, width, axis=dim)
        tail = lax.slice_in_dim(cells, cells.shape[dim] - width, cells.shape[dim], axis=dim)
        cells = jnp.concatenate(
            [
                lax.ppermute(tail, axis, [(i, (i + 1) % count) for i in range(count)]),
                cells,
                lax.ppermute(head, axis, [((i + 1) % count, i) for i in range(count)]),
            ],
            axis=dim,
        )
    return cells


def legendre_setup(wave_orders):
    colatitude = (jnp.arange(NLAT, dtype=jnp.float32) + 0.5) * (math.pi / NLAT)
    cosine = jnp.cos(colatitude)[None, :]
    order_col = wave_orders.astype(jnp.float32)[:, None]
    log_scale = (
        0.5
        * (
            jnp.log(2.0 * order_col + 1.0)
            - math.log(4.0 * math.pi)
            + lax.lgamma(2.0 * order_col + 1.0)
            - 2.0 * lax.lgamma(order_col + 1.0)
            - order_col * math.log(4.0)
        )
        + order_col * jnp.log(jnp.sin(colatitude))[None, :]
    )
    initial = jnp.exp(jnp.minimum(log_scale + 80.0, 0.0))
    restore = jnp.exp(jnp.maximum(log_scale, -80.0))
    quadrature = jnp.sin(colatitude) * (math.pi / NLAT) * (2.0 * math.pi / NLON)
    return (cosine, order_col, initial, restore, quadrature)


def legendre_step(degree, current, earlier, cosine, order_col, initial):
    square = degree * degree
    rising = jnp.sqrt(
        jnp.maximum(4.0 * square - 1.0, 1.0) / jnp.maximum(square - order_col * order_col, 1.0)
    )
    shifted = (degree - 1.0) * (degree - 1.0)
    falling = jnp.sqrt(
        jnp.maximum(shifted - order_col * order_col, 0.0) / jnp.maximum(4.0 * shifted - 1.0, 1.0)
    )
    advanced = rising * (cosine * current - falling * earlier)
    return jnp.where(degree < order_col, 0.0, jnp.where(degree == order_col, initial, advanced))


def legendre_tables(wave_orders):
    cosine, order_col, initial, restore, quadrature = legendre_setup(wave_orders)

    def advance(carry, base_degree):
        current, earlier = carry
        stacked = []
        for offset in range(unroll_steps):
            latest = legendre_step(
                (base_degree + offset).astype(jnp.float32),
                current,
                earlier,
                cosine,
                order_col,
                initial,
            )
            earlier = current
            current = latest
            stacked.append(latest * restore)
        return ((current, earlier), jnp.stack(stacked))

    zeroed = jnp.zeros((wave_orders.shape[0], NLAT), jnp.float32)
    _, pieces = lax.scan(advance, (zeroed, zeroed), jnp.arange(0, L, unroll_steps, dtype=jnp.int32))
    table = pieces.reshape(L, wave_orders.shape[0], NLAT)
    return ((table * quadrature[None, None, :]).astype(jnp.bfloat16), table.astype(jnp.bfloat16))


def fourier_table(wave_orders):
    longitude = jnp.arange(NLON, dtype=jnp.int32)
    phase = longitude[:, None] * wave_orders[None, :] % NLON
    angle = phase.astype(jnp.float32) * (2.0 * math.pi / NLON)
    paired = jnp.stack([jnp.cos(angle), -jnp.sin(angle)], axis=2)
    return paired.reshape(NLON, 2 * wave_orders.shape[0])


def to_bands(values):
    return lax.all_to_all(values, "lat", split_axis=2, concat_axis=0, tiled=True)


def regroup(values):
    return lax.all_to_all(values, "lon", split_axis=3, concat_axis=1, tiled=True)


def analyse(table_part, data_part, first_block, block_width):
    order_count = table_part.shape[1]
    channel_count = data_part.shape[1]

    def fill_block(block_index, accumulated):
        table_block = lax.dynamic_slice_in_dim(
            table_part, block_index * block_width, block_width, 0
        )
        partial_value = jnp.einsum(
            "lmt,tcmp->mcpl", table_block, data_part, preferred_element_type=jnp.float32
        )
        return lax.dynamic_update_slice_in_dim(
            accumulated, partial_value, block_index * block_width, 3
        )

    zeroed = jnp.zeros((order_count, channel_count, 2, L), jnp.float32)
    return lax.fori_loop(first_block, L // block_width, fill_block, zeroed)


def synthesise(table_part, data_part, first_block, block_width):
    order_count = table_part.shape[1]
    channel_count = data_part.shape[3]

    def add_block(block_index, accumulated):
        table_block = lax.dynamic_slice_in_dim(
            table_part, block_index * block_width, block_width, 0
        )
        degree_rows = lax.dynamic_slice_in_dim(data_part, block_index * block_width, block_width, 1)
        return accumulated + jnp.einsum(
            "lmt,mlpd->mpdt", table_block, degree_rows, preferred_element_type=jnp.float32
        )

    zeroed = jnp.zeros((order_count, 2, channel_count, NLAT), jnp.float32)
    return lax.fori_loop(first_block, L // block_width, add_block, zeroed)


def shards(cube_cells, block_source, block_weight, lift_in, lift_out, spectral):
    lat_count = lax.axis_size("lat")
    lon_count = lax.axis_size("lon")
    lat_index = lax.axis_index("lat")
    lon_index = lax.axis_index("lon")
    block_width = min(128, L)
    rim_tiles = SRC_DEV // 2
    per_band = L // lat_count
    half_size = per_band // 2
    slot_index = jnp.arange(per_band, dtype=jnp.int32)[None, :]
    band_index = jnp.arange(lat_count, dtype=jnp.int32)[:, None]
    all_orders = band_index * per_band + slot_index
    column_orders = all_orders.reshape(lat_count * per_band)
    own_orders = lax.dynamic_index_in_dim(all_orders, lat_index, 0, keepdims=False)
    table_wide = fourier_table(column_orders)
    forward = table_wide.astype(jnp.bfloat16)
    widened = extended(cube_cells, (("lon", 0),), rim_tiles)
    band_tiles = lon_count * SRC_DEV
    offsets = (block_source[:, 0, :] - lon_index * SRC_DEV + rim_tiles) % band_tiles
    picked = widened[offsets]
    remapped = jnp.einsum(
        "rkts,rkcs->rtc", block_weight[:, 0], picked, preferred_element_type=jnp.float32
    ).astype(jnp.bfloat16)
    hidden = jax.nn.gelu(
        jnp.einsum("rtc,cd->rtd", remapped, lift_in, preferred_element_type=jnp.float32)
    ).astype(jnp.bfloat16)
    lifted = jnp.einsum("rtd,de->ret", hidden, lift_out, preferred_element_type=jnp.float32).astype(
        jnp.bfloat16
    )
    grid_rows = lax.all_to_all(lifted, "lon", split_axis=1, concat_axis=2, tiled=True)
    spectra = jnp.einsum(
        "rcl,lq->rcq", grid_rows, forward, preferred_element_type=jnp.float32
    ).astype(jnp.bfloat16)
    gathered = to_bands(spectra)
    channel_count = gathered.shape[1]
    gathered = gathered.reshape(NLAT, channel_count, per_band, 2)
    weighted, plain_table = legendre_tables(own_orders)
    sections = []
    for half_index in range(2):
        lowest = half_index * half_size
        first_block = own_orders[lowest] // block_width
        sections.append(
            analyse(
                weighted[:, lowest : lowest + half_size, :],
                gathered[:, :, lowest : lowest + half_size, :],
                first_block,
                block_width,
            )
        )
    analysis = jnp.concatenate(sections, axis=0).astype(jnp.bfloat16)
    by_degree = regroup(analysis)
    mixed_modes = jnp.einsum(
        "mcpl,lcd->mlpd", by_degree, spectral, preferred_element_type=jnp.float32
    ).astype(jnp.bfloat16)
    returned = regroup(mixed_modes)
    pieces = []
    for half_index in range(2):
        lowest = half_index * half_size
        first_block = own_orders[lowest] // block_width
        pieces.append(
            synthesise(
                plain_table[:, lowest : lowest + half_size, :],
                returned[lowest : lowest + half_size],
                first_block,
                block_width,
            )
        )
    synthesized = (
        jnp.concatenate(pieces, axis=0)
        .astype(jnp.bfloat16)
        .reshape(2 * per_band, channel_count, NLAT)
    )
    rows_back = to_bands(synthesized)
    factors = jnp.repeat(jnp.where(column_orders == 0, 1.0, 2.0), 2).astype(jnp.bfloat16)
    inverse = forward * factors[None, :]
    grid_field = jnp.einsum(
        "qcr,kq->rkc", rows_back, inverse, preferred_element_type=jnp.float32
    ).astype(jnp.bfloat16)
    return lax.all_to_all(grid_field, "lon", split_axis=1, concat_axis=2, tiled=True)


PARTS = 3
PAIRS = 3
STEP = 16
F32 = jnp.float32
BF16 = jnp.bfloat16


def params():
    return pltpu.CompilerParams(vmem_limit_bytes=56 * 1024 * 1024)


def cost(flops, moved):
    return pl.CostEstimate(flops=flops, bytes_accessed=moved, transcendentals=0)


def whole_block(shape):
    zeros = (0,) * len(shape)
    return pl.BlockSpec(shape, lambda *_: zeros)


def halves(left, right, at):
    return jnp.concatenate([left[:, at : at + 64], right[:, at : at + 64]], axis=1)


def lift_kernel(first_row, picks, tiles, weight, lift_in, lift_out, *outs):
    rows = []
    for r in range(2):
        row = first_row + pl.program_id(0) * 2 + r
        source = jnp.concatenate([tiles[picks[row * 4 + k]] for k in range(4)], axis=1)
        blocks = jnp.concatenate([weight[r, k] for k in range(4)], axis=1)
        remapped = lax.dot_general(
            blocks, source, (((1,), (1,)), ((), ())), preferred_element_type=F32
        ).astype(BF16)
        hidden = jax.nn.gelu(jnp.dot(remapped, lift_in[...], preferred_element_type=F32))
        rows.append(
            jnp.dot(hidden.astype(BF16), lift_out[...], preferred_element_type=F32).astype(BF16)
        )
    for q in range(4):
        outs[q][0] = halves(rows[0], rows[1], 64 * q)


def lift_part(part, pairs, picks, tiles, weight, lift_in, lift_out):
    width = weight.shape[2]
    return pl.pallas_call(
        lambda *refs: lift_kernel(part * pairs * 2, *refs),
        out_shape=[jax.ShapeDtypeStruct((pairs, width, 128), BF16)] * 4,
        grid_spec=pltpu.PrefetchScalarGridSpec(
            num_scalar_prefetch=1,
            grid=(pairs,),
            in_specs=[
                whole_block(tiles.shape),
                pl.BlockSpec((2, 4, width, 128), lambda g, _: (part * pairs + g, 0, 0, 0)),
                whole_block(lift_in.shape),
                whole_block(lift_out.shape),
            ],
            out_specs=[pl.BlockSpec((1, width, 128), lambda g, _: (g, 0, 0))] * 4,
        ),
        compiler_params=params(),
        cost_estimate=cost(pairs * 2 * width * 256 * 256 * 4, pairs * width * 128 * 24),
        name="lift_rows",
    )(picks, tiles, weight, lift_in, lift_out)


def dft_kernel(table, scale, first, second, third, fourth, out):
    data = (first, second, third, fourth)
    total = None
    for j in range(4):
        block = jnp.concatenate([data[j][g] for g in range(PAIRS)], axis=1)
        term = jnp.dot(table[j], block, preferred_element_type=F32)
        total = term if total is None else total + term
    total = total * scale[0]
    half = total.shape[0] // 2
    orders = half // 8
    for r in range(2 * PAIRS):
        row = halves(total[:half], total[half:], 64 * r).astype(BF16)
        for i in range(8):
            out[i, r] = row[i * orders : (i + 1) * orders]


def dft_part(table, data, scale):
    pairs, width, _ = data[0].shape
    waves = table.shape[1]
    rows = 2 * PAIRS
    return pl.pallas_call(
        dft_kernel,
        out_shape=jax.ShapeDtypeStruct((8, 2 * pairs, waves // 16, 128), BF16),
        grid=(pairs // PAIRS,),
        in_specs=[
            whole_block(table.shape),
            pl.BlockSpec((1, 1, 64 * rows), lambda g: (g, 0, 0)),
        ]
        + [pl.BlockSpec((PAIRS, width, 128), lambda g: (g, 0, 0))] * 4,
        out_specs=pl.BlockSpec((8, rows, waves // 16, 128), lambda g: (0, g, 0, 0)),
        compiler_params=params(),
        cost_estimate=cost(pairs * 128 * 4 * width * waves * 2, pairs * 128 * 4 * width * 4),
        name="forward_rows",
    )(table, scale, *data)


def legendre_kernel(cosine, order, initial, restore, out, current, earlier, held):
    base = pl.program_id(0) * STEP

    @pl.when(base == 0)
    def _():
        current[...] = jnp.zeros_like(current)
        earlier[...] = jnp.zeros_like(earlier)

    orders = order.shape[0]
    now, before = current[...], earlier[...]
    for s in range(STEP):
        degree = (base + s).astype(F32)
        square = degree * degree
        order_square = order[...] * order[...]
        rising = jnp.sqrt(
            jnp.maximum(4.0 * square - 1.0, 1.0) / jnp.maximum(square - order_square, 1.0)
        )
        shifted = (degree - 1.0) * (degree - 1.0)
        falling = jnp.sqrt(
            jnp.maximum(shifted - order_square, 0.0) / jnp.maximum(4.0 * shifted - 1.0, 1.0)
        )
        advanced = rising * (cosine[...] * now - falling * before)
        latest = jnp.where(
            degree < order[...], 0.0, jnp.where(degree == order[...], initial[...], advanced)
        )
        now, before = latest, now
        held[s] = latest * restore[...]
    current[...] = now
    earlier[...] = before
    out[...] = jnp.swapaxes(held[...], 0, 1)[:, :, : out.shape[2]].astype(BF16)


def legendre_table(orders, row_order):
    cosine, order_col, initial, restore, quadrature = legendre_setup(orders)
    extra = ((0, 0), (0, -NLAT % 128))
    cosine, initial, restore = (
        jnp.pad(value[:, row_order], extra) for value in (cosine, initial, restore)
    )
    count, wide = initial.shape
    table = pl.pallas_call(
        legendre_kernel,
        out_shape=jax.ShapeDtypeStruct((count, L, NLAT), BF16),
        grid=(L // STEP,),
        in_specs=[
            whole_block((1, wide)),
            whole_block((count, 1)),
            whole_block((count, wide)),
            whole_block((count, wide)),
        ],
        out_specs=pl.BlockSpec((count, STEP, NLAT), lambda g: (0, g, 0)),
        scratch_shapes=[
            pltpu.VMEM((count, wide), F32),
            pltpu.VMEM((count, wide), F32),
            pltpu.VMEM((STEP, count, wide), F32),
        ],
        compiler_params=params(),
        cost_estimate=cost(L * count * wide * 100, count * L * NLAT * 2),
        name="legendre_table",
    )(cosine, order_col, initial, restore)
    return table, quadrature


def analysis_kernel(table, first, second, third, out):
    for m in range(table.shape[0]):
        rows = jnp.concatenate([first[m], second[m], third[m]], axis=0)
        out[m] = jnp.dot(table[m], rows, preferred_element_type=F32).astype(BF16)


def analysis_all(table, pieces, group=4):
    count = table.shape[0]
    depth = pieces[0].shape[1]
    return pl.pallas_call(
        analysis_kernel,
        out_shape=jax.ShapeDtypeStruct((count, L, 128), BF16),
        grid=(count // group,),
        in_specs=[pl.BlockSpec((group, L, NLAT), lambda g: (g, 0, 0))]
        + [pl.BlockSpec((group, depth, 128), lambda g: (g, 0, 0))] * 3,
        out_specs=pl.BlockSpec((group, L, 128), lambda g: (g, 0, 0)),
        compiler_params=params(),
        cost_estimate=cost(count * L * NLAT * 256, count * L * NLAT * 2),
        name="analysis",
    )(table, *pieces)


def mix_kernel(data, matrix, out):
    for l in range(data.shape[1]):
        sides = []
        for p in range(2):
            sides.append(
                jnp.concatenate([data[j, l][:, 64 * p : 64 * p + 64] for j in range(4)], axis=1)
            )
        joined = jnp.concatenate(sides, axis=0)
        mixed = jnp.dot(joined, matrix[l], preferred_element_type=F32).astype(BF16)
        count = data.shape[2]
        for q in range(4):
            out[q, l] = halves(mixed[:count], mixed[count:], 64 * q)


def mix_all(data, matrix, group=8):
    _, degrees, count, _ = data.shape
    spec = pl.BlockSpec((4, group, count, 128), lambda g: (0, g, 0, 0))
    return pl.pallas_call(
        mix_kernel,
        out_shape=jax.ShapeDtypeStruct(data.shape, BF16),
        grid=(degrees // group,),
        in_specs=[spec, pl.BlockSpec((group, 256, 256), lambda g: (g, 0, 0))],
        out_specs=spec,
        compiler_params=params(),
        cost_estimate=cost(degrees * count * 4 * 256 * 256, degrees * 256 * 256 * 2),
        name="mixing",
    )(data, matrix)


def synthesis_kernel(table, data, first, second, third):
    for m in range(table.shape[0]):
        value = lax.dot_general(
            table[m], data[m], (((0,), (0,)), ((), ())), preferred_element_type=F32
        ).astype(BF16)
        depth = first.shape[1]
        first[m] = value[:depth]
        second[m] = value[depth : 2 * depth]
        third[m] = value[2 * depth :]


def synthesis_all(table, data, group=4):
    count = table.shape[0]
    depth = NLAT // PARTS
    return pl.pallas_call(
        synthesis_kernel,
        out_shape=[jax.ShapeDtypeStruct((count, depth, 128), BF16)] * 3,
        grid=(count // group,),
        in_specs=[
            pl.BlockSpec((group, L, NLAT), lambda g: (g, 0, 0)),
            pl.BlockSpec((group, L, 128), lambda g: (g, 0, 0)),
        ],
        out_specs=[pl.BlockSpec((group, depth, 128), lambda g: (g, 0, 0))] * 3,
        compiler_params=params(),
        cost_estimate=cost(count * L * NLAT * 256, count * L * NLAT * 2),
        name="synthesis",
    )(table, data)


def inverse_kernel(table, data, *outs):
    columns = [[], []]
    for r in range(2 * PAIRS):
        row = jnp.concatenate([data[i, r] for i in range(8)], axis=0)
        for p in range(2):
            columns[p].append(row[:, 64 * p : 64 * p + 64])
    joined = jnp.concatenate([jnp.concatenate(side, axis=1) for side in columns], axis=0)
    for j in range(4):
        value = jnp.dot(table[j], joined, preferred_element_type=F32).astype(BF16)
        for g in range(PAIRS):
            outs[j][g] = value[:, 128 * g : 128 * g + 128]


def inverse_part(table, data):
    _, rows, orders, _ = data.shape
    width = table.shape[1]
    return pl.pallas_call(
        inverse_kernel,
        out_shape=[jax.ShapeDtypeStruct((rows // 2, width, 128), BF16)] * 4,
        grid=(rows // (2 * PAIRS),),
        in_specs=[
            whole_block(table.shape),
            pl.BlockSpec((8, 2 * PAIRS, orders, 128), lambda g: (0, g, 0, 0)),
        ],
        out_specs=[pl.BlockSpec((PAIRS, width, 128), lambda g: (g, 0, 0))] * 4,
        compiler_params=params(),
        cost_estimate=cost(rows * 64 * 4 * width * 16 * orders * 2, rows * 64 * 4 * width * 4),
        name="inverse_rows",
    )(table, data)


def join_kernel(place, *refs):
    data, out = refs[:4], refs[-1]
    for here in range(4):

        @pl.when(place[0] == here)
        def _():
            blocks = [data[here ^ j][0] for j in range(4)]
            for r in range(2):
                out[r] = jnp.concatenate(
                    [block[:, 64 * r : 64 * r + 64] for block in blocks], axis=1
                )


def join_part(part, place, data, prior):
    pairs, width, _ = data[0].shape
    first = prior is None
    return pl.pallas_call(
        join_kernel,
        out_shape=jax.ShapeDtypeStruct((2 * pairs * PARTS, width, 256), BF16),
        grid_spec=pltpu.PrefetchScalarGridSpec(
            num_scalar_prefetch=1,
            grid=(pairs,),
            in_specs=[pl.BlockSpec((1, width, 128), lambda g, _: (g, 0, 0))] * 4
            + ([] if first else [pl.BlockSpec(memory_space=pl.ANY)]),
            out_specs=pl.BlockSpec((2, width, 256), lambda g, _: (part * pairs + g, 0, 0)),
        ),
        input_output_aliases={} if first else {5: 0},
        compiler_params=params(),
        cost_estimate=cost(0, pairs * width * 256 * 8),
        name="join_rows",
    )(place, *data, *(() if first else (prior,)))


def exchange(pieces, axis):
    count = lax.axis_size(axis)
    return [pieces[0]] + [
        lax.ppermute(pieces[s], axis, [(i, i ^ s) for i in range(count)])
        for s in range(1, count)
    ]


def swap(values, axis):
    return lax.all_to_all(values, axis, split_axis=0, concat_axis=0, tiled=True)


def fourier_pair(blocks):
    orders = jnp.arange(L, dtype=jnp.int32)
    width = NLON // blocks.shape[0]
    longitude = blocks[:, None, None] * width + jnp.arange(width, dtype=jnp.int32)
    phase = (longitude * orders[None, :, None]) % NLON
    angle = phase.astype(F32) * (2.0 * math.pi / NLON)
    forward = jnp.concatenate([jnp.cos(angle), -jnp.sin(angle)], axis=1).astype(BF16)
    factor = jnp.where(orders == 0, 1.0, 2.0).astype(BF16)
    inverse = forward * jnp.tile(factor, 2)[None, :, None]
    return forward, jnp.swapaxes(inverse, 1, 2)


def packed_shards(cube_cells, block_source, block_weight, lift_in, lift_out, spectral):
    lat_count = lax.axis_size("lat")
    lon_count = lax.axis_size("lon")
    lon_index = lax.axis_index("lon")
    rows = block_weight.shape[0]
    pairs = rows // (2 * PARTS)
    per_band = L // lat_count
    rim_tiles = SRC_DEV // 2
    own_orders = lax.axis_index("lat") * per_band + jnp.arange(per_band, dtype=jnp.int32)

    widened = extended(cube_cells, (("lon", 0),), rim_tiles)
    picks = (block_source[:, 0, :] - lon_index * SRC_DEV + rim_tiles) % (lon_count * SRC_DEV)
    picks = picks.reshape(-1)
    weight = block_weight[:, 0]
    blocks = lon_index ^ jnp.arange(lon_count, dtype=jnp.int32)
    forward, inverse = fourier_pair(blocks)
    lift_out = lift_out.reshape(-1, lon_count, 64)[:, blocks].reshape(lift_out.shape)
    place = lon_index.astype(jnp.int32).reshape(1)
    row_order = jnp.arange(NLAT, dtype=jnp.int32).reshape(lat_count, PARTS, 2 * pairs)
    row_order = jnp.swapaxes(row_order, 0, 1).reshape(NLAT)
    table, quadrature = legendre_table(own_orders, row_order)
    own_scale = lax.dynamic_slice_in_dim(quadrature, lax.axis_index("lat") * rows, rows)
    own_scale = jnp.repeat(own_scale, 64).reshape(PARTS, pairs // PAIRS, 1, 128 * PAIRS)

    pieces = []
    for part in range(PARTS):
        lifted = lift_part(part, pairs, picks, widened, weight, lift_in, lift_out)
        if part:
            lifted, _ = lax.optimization_barrier((lifted, arrived))
        arrived = exchange(lifted, "lon")
        spectra = dft_part(forward, arrived, own_scale[part])
        gathered = swap(spectra, "lat").reshape(NLAT // PARTS, per_band, 128)
        pieces.append(jnp.swapaxes(gathered, 0, 1))
    analysis = analysis_all(table, pieces)
    split = analysis.reshape(per_band, lon_count, L // lon_count, 128)
    by_degree = swap(jnp.transpose(split, (1, 2, 0, 3)), "lon")
    returned = swap(mix_all(by_degree, spectral), "lon").reshape(L, per_band, 128)
    synthesized = synthesis_all(table, jnp.swapaxes(returned, 0, 1))
    grid_field = None
    for part in range(PARTS):
        sent = jnp.swapaxes(synthesized[part], 0, 1)
        sent = sent.reshape(lat_count, 2 * pairs, per_band, 128)
        placed = inverse_part(inverse, swap(sent, "lat"))
        grid_field = join_part(part, place, exchange(placed, "lon"), grid_field)
    return grid_field


def solution(mesh):
    packed = mesh.shape["lat"] == 8 and mesh.shape["lon"] == 4
    in_specs = (
        P(("lat", "lon"), None, None),
        P("lat", "lon", None),
        P("lat", "lon", None, None, None),
        P(),
        P(),
        P("lon", None, None),
    )
    out_specs = P("lat", "lon", None)
    return jax.shard_map(packed_shards if packed else shards, mesh=mesh, in_specs=in_specs, out_specs=out_specs, check_vma=False)
```

```python
import math

import jax
import jax.numpy as jnp
from jax import lax
from jax.experimental import pallas as pl
from jax.experimental.pallas import tpu as pltpu
from jax.sharding import PartitionSpec as P

NLAT = 720
NLON = 1440
L = 384
SRC_DEV = 48


unroll_steps = 16


def extended(cells, sides, width):
    for axis, dim in sides:
        count = lax.axis_size(axis)
        head = lax.slice_in_dim(cells, 0, width, axis=dim)
        tail = lax.slice_in_dim(cells, cells.shape[dim] - width, cells.shape[dim], axis=dim)
        cells = jnp.concatenate(
            [
                lax.ppermute(tail, axis, [(i, (i + 1) % count) for i in range(count)]),
                cells,
                lax.ppermute(head, axis, [((i + 1) % count, i) for i in range(count)]),
            ],
            axis=dim,
        )
    return cells


def legendre_setup(wave_orders):
    colatitude = (jnp.arange(NLAT, dtype=jnp.float32) + 0.5) * (math.pi / NLAT)
    cosine = jnp.cos(colatitude)[None, :]
    order_col = wave_orders.astype(jnp.float32)[:, None]
    log_scale = (
        0.5
        * (
            jnp.log(2.0 * order_col + 1.0)
            - math.log(4.0 * math.pi)
            + lax.lgamma(2.0 * order_col + 1.0)
            - 2.0 * lax.lgamma(order_col + 1.0)
            - order_col * math.log(4.0)
        )
        + order_col * jnp.log(jnp.sin(colatitude))[None, :]
    )
    initial = jnp.exp(jnp.minimum(log_scale + 80.0, 0.0))
    restore = jnp.exp(jnp.maximum(log_scale, -80.0))
    quadrature = jnp.sin(colatitude) * (math.pi / NLAT) * (2.0 * math.pi / NLON)
    return (cosine, order_col, initial, restore, quadrature)


def legendre_step(degree, current, earlier, cosine, order_col, initial):
    square = degree * degree
    rising = jnp.sqrt(
        jnp.maximum(4.0 * square - 1.0, 1.0) / jnp.maximum(square - order_col * order_col, 1.0)
    )
    shifted = (degree - 1.0) * (degree - 1.0)
    falling = jnp.sqrt(
        jnp.maximum(shifted - order_col * order_col, 0.0) / jnp.maximum(4.0 * shifted - 1.0, 1.0)
    )
    advanced = rising * (cosine * current - falling * earlier)
    return jnp.where(degree < order_col, 0.0, jnp.where(degree == order_col, initial, advanced))


def legendre_tables(wave_orders):
    cosine, order_col, initial, restore, quadrature = legendre_setup(wave_orders)

    def advance(carry, base_degree):
        current, earlier = carry
        stacked = []
        for offset in range(unroll_steps):
            latest = legendre_step(
                (base_degree + offset).astype(jnp.float32),
                current,
                earlier,
                cosine,
                order_col,
                initial,
            )
            earlier = current
            current = latest
            stacked.append(latest * restore)
        return ((current, earlier), jnp.stack(stacked))

    zeroed = jnp.zeros((wave_orders.shape[0], NLAT), jnp.float32)
    _, pieces = lax.scan(advance, (zeroed, zeroed), jnp.arange(0, L, unroll_steps, dtype=jnp.int32))
    table = pieces.reshape(L, wave_orders.shape[0], NLAT)
    return ((table * quadrature[None, None, :]).astype(jnp.bfloat16), table.astype(jnp.bfloat16))


def fourier_table(wave_orders):
    longitude = jnp.arange(NLON, dtype=jnp.int32)
    phase = longitude[:, None] * wave_orders[None, :] % NLON
    angle = phase.astype(jnp.float32) * (2.0 * math.pi / NLON)
    paired = jnp.stack([jnp.cos(angle), -jnp.sin(angle)], axis=2)
    return paired.reshape(NLON, 2 * wave_orders.shape[0])


def to_bands(values):
    return lax.all_to_all(values, "lat", split_axis=2, concat_axis=0, tiled=True)


def regroup(values):
    return lax.all_to_all(values, "lon", split_axis=3, concat_axis=1, tiled=True)


def analyse(table_part, data_part, first_block, block_width):
    order_count = table_part.shape[1]
    channel_count = data_part.shape[1]

    def fill_block(block_index, accumulated):
        table_block = lax.dynamic_slice_in_dim(
            table_part, block_index * block_width, block_width, 0
        )
        partial_value = jnp.einsum(
            "lmt,tcmp->mcpl", table_block, data_part, preferred_element_type=jnp.float32
        )
        return lax.dynamic_update_slice_in_dim(
            accumulated, partial_value, block_index * block_width, 3
        )

    zeroed = jnp.zeros((order_count, channel_count, 2, L), jnp.float32)
    return lax.fori_loop(first_block, L // block_width, fill_block, zeroed)


def synthesise(table_part, data_part, first_block, block_width):
    order_count = table_part.shape[1]
    channel_count = data_part.shape[3]

    def add_block(block_index, accumulated):
        table_block = lax.dynamic_slice_in_dim(
            table_part, block_index * block_width, block_width, 0
        )
        degree_rows = lax.dynamic_slice_in_dim(data_part, block_index * block_width, block_width, 1)
        return accumulated + jnp.einsum(
            "lmt,mlpd->mpdt", table_block, degree_rows, preferred_element_type=jnp.float32
        )

    zeroed = jnp.zeros((order_count, 2, channel_count, NLAT), jnp.float32)
    return lax.fori_loop(first_block, L // block_width, add_block, zeroed)


def shards(cube_cells, block_source, block_weight, lift_in, lift_out, spectral):
    lat_count = lax.axis_size("lat")
    lon_count = lax.axis_size("lon")
    lat_index = lax.axis_index("lat")
    lon_index = lax.axis_index("lon")
    block_width = min(128, L)
    rim_tiles = SRC_DEV // 2
    per_band = L // lat_count
    half_size = per_band // 2
    slot_index = jnp.arange(per_band, dtype=jnp.int32)[None, :]
    band_index = jnp.arange(lat_count, dtype=jnp.int32)[:, None]
    all_orders = band_index * per_band + slot_index
    column_orders = all_orders.reshape(lat_count * per_band)
    own_orders = lax.dynamic_index_in_dim(all_orders, lat_index, 0, keepdims=False)
    table_wide = fourier_table(column_orders)
    forward = table_wide.astype(jnp.bfloat16)
    widened = extended(cube_cells, (("lon", 0),), rim_tiles)
    band_tiles = lon_count * SRC_DEV
    offsets = (block_source[:, 0, :] - lon_index * SRC_DEV + rim_tiles) % band_tiles
    picked = widened[offsets]
    remapped = jnp.einsum(
        "rkts,rkcs->rtc", block_weight[:, 0], picked, preferred_element_type=jnp.float32
    ).astype(jnp.bfloat16)
    hidden = jax.nn.gelu(
        jnp.einsum("rtc,cd->rtd", remapped, lift_in, preferred_element_type=jnp.float32)
    ).astype(jnp.bfloat16)
    lifted = jnp.einsum("rtd,de->ret", hidden, lift_out, preferred_element_type=jnp.float32).astype(
        jnp.bfloat16
    )
    grid_rows = lax.all_to_all(lifted, "lon", split_axis=1, concat_axis=2, tiled=True)
    spectra = jnp.einsum(
        "rcl,lq->rcq", grid_rows, forward, preferred_element_type=jnp.float32
    ).astype(jnp.bfloat16)
    gathered = to_bands(spectra)
    channel_count = gathered.shape[1]
    gathered = gathered.reshape(NLAT, channel_count, per_band, 2)
    weighted, plain_table = legendre_tables(own_orders)
    sections = []
    for half_index in range(2):
        lowest = half_index * half_size
        first_block = own_orders[lowest] // block_width
        sections.append(
            analyse(
                weighted[:, lowest : lowest + half_size, :],
                gathered[:, :, lowest : lowest + half_size, :],
                first_block,
                block_width,
            )
        )
    analysis = jnp.concatenate(sections, axis=0).astype(jnp.bfloat16)
    by_degree = regroup(analysis)
    mixed_modes = jnp.einsum(
        "mcpl,lcd->mlpd", by_degree, spectral, preferred_element_type=jnp.float32
    ).astype(jnp.bfloat16)
    returned = regroup(mixed_modes)
    pieces = []
    for half_index in range(2):
        lowest = half_index * half_size
        first_block = own_orders[lowest] // block_width
        pieces.append(
            synthesise(
                plain_table[:, lowest : lowest + half_size, :],
                returned[lowest : lowest + half_size],
                first_block,
                block_width,
            )
        )
    synthesized = (
        jnp.concatenate(pieces, axis=0)
        .astype(jnp.bfloat16)
        .reshape(2 * per_band, channel_count, NLAT)
    )
    rows_back = to_bands(synthesized)
    factors = jnp.repeat(jnp.where(column_orders == 0, 1.0, 2.0), 2).astype(jnp.bfloat16)
    inverse = forward * factors[None, :]
    grid_field = jnp.einsum(
        "qcr,kq->rkc", rows_back, inverse, preferred_element_type=jnp.float32
    ).astype(jnp.bfloat16)
    return lax.all_to_all(grid_field, "lon", split_axis=1, concat_axis=2, tiled=True)


PARTS = 3
PAIRS = 3
STEP = 16
F32 = jnp.float32
BF16 = jnp.bfloat16


def params():
    return pltpu.CompilerParams(vmem_limit_bytes=56 * 1024 * 1024)


def cost(flops, moved):
    return pl.CostEstimate(flops=flops, bytes_accessed=moved, transcendentals=0)


def whole_block(shape):
    zeros = (0,) * len(shape)
    return pl.BlockSpec(shape, lambda *_: zeros)


def halves(left, right, at):
    return jnp.concatenate([left[:, at : at + 64], right[:, at : at + 64]], axis=1)


def lift_kernel(first_row, picks, tiles, weight, lift_in, lift_out, *outs):
    rows = []
    for r in range(2):
        row = first_row + pl.program_id(0) * 2 + r
        source = jnp.concatenate([tiles[picks[row * 4 + k]] for k in range(4)], axis=1)
        blocks = jnp.concatenate([weight[r, k] for k in range(4)], axis=1)
        remapped = lax.dot_general(
            blocks, source, (((1,), (1,)), ((), ())), preferred_element_type=F32
        ).astype(BF16)
        hidden = jax.nn.gelu(jnp.dot(remapped, lift_in[...], preferred_element_type=F32))
        rows.append(
            jnp.dot(hidden.astype(BF16), lift_out[...], preferred_element_type=F32).astype(BF16)
        )
    for q in range(4):
        outs[q][0] = halves(rows[0], rows[1], 64 * q)


def lift_part(part, pairs, picks, tiles, weight, lift_in, lift_out):
    width = weight.shape[2]
    return pl.pallas_call(
        lambda *refs: lift_kernel(part * pairs * 2, *refs),
        out_shape=[jax.ShapeDtypeStruct((pairs, width, 128), BF16)] * 4,
        grid_spec=pltpu.PrefetchScalarGridSpec(
            num_scalar_prefetch=1,
            grid=(pairs,),
            in_specs=[
                whole_block(tiles.shape),
                pl.BlockSpec((2, 4, width, 128), lambda g, _: (part * pairs + g, 0, 0, 0)),
                whole_block(lift_in.shape),
                whole_block(lift_out.shape),
            ],
            out_specs=[pl.BlockSpec((1, width, 128), lambda g, _: (g, 0, 0))] * 4,
        ),
        compiler_params=params(),
        cost_estimate=cost(pairs * 2 * width * 256 * 256 * 4, pairs * width * 128 * 24),
        name="lift_rows",
    )(picks, tiles, weight, lift_in, lift_out)


def dft_kernel(table, scale, first, second, third, fourth, out):
    data = (first, second, third, fourth)
    total = None
    for j in range(4):
        block = jnp.concatenate([data[j][g] for g in range(PAIRS)], axis=1)
        term = jnp.dot(table[j], block, preferred_element_type=F32)
        total = term if total is None else total + term
    total = total * scale[0]
    half = total.shape[0] // 2
    orders = half // 8
    for r in range(2 * PAIRS):
        row = halves(total[:half], total[half:], 64 * r).astype(BF16)
        for i in range(8):
            out[i, r] = row[i * orders : (i + 1) * orders]


def dft_part(table, data, scale):
    pairs, width, _ = data[0].shape
    waves = table.shape[1]
    rows = 2 * PAIRS
    return pl.pallas_call(
        dft_kernel,
        out_shape=jax.ShapeDtypeStruct((8, 2 * pairs, waves // 16, 128), BF16),
        grid=(pairs // PAIRS,),
        in_specs=[
            whole_block(table.shape),
            pl.BlockSpec((1, 1, 64 * rows), lambda g: (g, 0, 0)),
        ]
        + [pl.BlockSpec((PAIRS, width, 128), lambda g: (g, 0, 0))] * 4,
        out_specs=pl.BlockSpec((8, rows, waves // 16, 128), lambda g: (0, g, 0, 0)),
        compiler_params=params(),
        cost_estimate=cost(pairs * 128 * 4 * width * waves * 2, pairs * 128 * 4 * width * 4),
        name="forward_rows",
    )(table, scale, *data)


def legendre_kernel(cosine, order, initial, restore, out, current, earlier, held):
    base = pl.program_id(0) * STEP

    @pl.when(base == 0)
    def _():
        current[...] = jnp.zeros_like(current)
        earlier[...] = jnp.zeros_like(earlier)

    orders = order.shape[0]
    now, before = current[...], earlier[...]
    for s in range(STEP):
        degree = (base + s).astype(F32)
        square = degree * degree
        order_square = order[...] * order[...]
        rising = jnp.sqrt(
            jnp.maximum(4.0 * square - 1.0, 1.0) / jnp.maximum(square - order_square, 1.0)
        )
        shifted = (degree - 1.0) * (degree - 1.0)
        falling = jnp.sqrt(
            jnp.maximum(shifted - order_square, 0.0) / jnp.maximum(4.0 * shifted - 1.0, 1.0)
        )
        advanced = rising * (cosine[...] * now - falling * before)
        latest = jnp.where(
            degree < order[...], 0.0, jnp.where(degree == order[...], initial[...], advanced)
        )
        now, before = latest, now
        held[s] = latest * restore[...]
    current[...] = now
    earlier[...] = before
    out[...] = jnp.swapaxes(held[...], 0, 1)[:, :, : out.shape[2]].astype(BF16)


def legendre_table(orders, row_order):
    cosine, order_col, initial, restore, quadrature = legendre_setup(orders)
    extra = ((0, 0), (0, -NLAT % 128))
    cosine, initial, restore = (
        jnp.pad(value[:, row_order], extra) for value in (cosine, initial, restore)
    )
    count, wide = initial.shape
    table = pl.pallas_call(
        legendre_kernel,
        out_shape=jax.ShapeDtypeStruct((count, L, NLAT), BF16),
        grid=(L // STEP,),
        in_specs=[
            whole_block((1, wide)),
            whole_block((count, 1)),
            whole_block((count, wide)),
            whole_block((count, wide)),
        ],
        out_specs=pl.BlockSpec((count, STEP, NLAT), lambda g: (0, g, 0)),
        scratch_shapes=[
            pltpu.VMEM((count, wide), F32),
            pltpu.VMEM((count, wide), F32),
            pltpu.VMEM((STEP, count, wide), F32),
        ],
        compiler_params=params(),
        cost_estimate=cost(L * count * wide * 100, count * L * NLAT * 2),
        name="legendre_table",
    )(cosine, order_col, initial, restore)
    return table, quadrature


def analysis_kernel(table, first, second, third, out):
    for m in range(table.shape[0]):
        rows = jnp.concatenate([first[m], second[m], third[m]], axis=0)
        out[m] = jnp.dot(table[m], rows, preferred_element_type=F32).astype(BF16)


def analysis_all(table, pieces, group=4):
    count = table.shape[0]
    depth = pieces[0].shape[1]
    return pl.pallas_call(
        analysis_kernel,
        out_shape=jax.ShapeDtypeStruct((count, L, 128), BF16),
        grid=(count // group,),
        in_specs=[pl.BlockSpec((group, L, NLAT), lambda g: (g, 0, 0))]
        + [pl.BlockSpec((group, depth, 128), lambda g: (g, 0, 0))] * 3,
        out_specs=pl.BlockSpec((group, L, 128), lambda g: (g, 0, 0)),
        compiler_params=params(),
        cost_estimate=cost(count * L * NLAT * 256, count * L * NLAT * 2),
        name="analysis",
    )(table, *pieces)


def mix_kernel(data, matrix, out):
    for l in range(data.shape[1]):
        sides = []
        for p in range(2):
            sides.append(
                jnp.concatenate([data[j, l][:, 64 * p : 64 * p + 64] for j in range(4)], axis=1)
            )
        joined = jnp.concatenate(sides, axis=0)
        mixed = jnp.dot(joined, matrix[l], preferred_element_type=F32).astype(BF16)
        count = data.shape[2]
        for q in range(4):
            out[q, l] = halves(mixed[:count], mixed[count:], 64 * q)


def mix_all(data, matrix, group=8):
    _, degrees, count, _ = data.shape
    spec = pl.BlockSpec((4, group, count, 128), lambda g: (0, g, 0, 0))
    return pl.pallas_call(
        mix_kernel,
        out_shape=jax.ShapeDtypeStruct(data.shape, BF16),
        grid=(degrees // group,),
        in_specs=[spec, pl.BlockSpec((group, 256, 256), lambda g: (g, 0, 0))],
        out_specs=spec,
        compiler_params=params(),
        cost_estimate=cost(degrees * count * 4 * 256 * 256, degrees * 256 * 256 * 2),
        name="mixing",
    )(data, matrix)


def synthesis_kernel(table, data, first, second, third):
    for m in range(table.shape[0]):
        value = lax.dot_general(
            table[m], data[m], (((0,), (0,)), ((), ())), preferred_element_type=F32
        ).astype(BF16)
        depth = first.shape[1]
        first[m] = value[:depth]
        second[m] = value[depth : 2 * depth]
        third[m] = value[2 * depth :]


def synthesis_all(table, data, group=4):
    count = table.shape[0]
    depth = NLAT // PARTS
    return pl.pallas_call(
        synthesis_kernel,
        out_shape=[jax.ShapeDtypeStruct((count, depth, 128), BF16)] * 3,
        grid=(count // group,),
        in_specs=[
            pl.BlockSpec((group, L, NLAT), lambda g: (g, 0, 0)),
            pl.BlockSpec((group, L, 128), lambda g: (g, 0, 0)),
        ],
        out_specs=[pl.BlockSpec((group, depth, 128), lambda g: (g, 0, 0))] * 3,
        compiler_params=params(),
        cost_estimate=cost(count * L * NLAT * 256, count * L * NLAT * 2),
        name="synthesis",
    )(table, data)


def inverse_kernel(table, data, *outs):
    columns = [[], []]
    for r in range(2 * PAIRS):
        row = jnp.concatenate([data[i, r] for i in range(8)], axis=0)
        for p in range(2):
            columns[p].append(row[:, 64 * p : 64 * p + 64])
    joined = jnp.concatenate([jnp.concatenate(side, axis=1) for side in columns], axis=0)
    for j in range(4):
        value = jnp.dot(table[j], joined, preferred_element_type=F32).astype(BF16)
        for g in range(PAIRS):
            outs[j][g] = value[:, 128 * g : 128 * g + 128]


def inverse_part(table, data):
    _, rows, orders, _ = data.shape
    width = table.shape[1]
    return pl.pallas_call(
        inverse_kernel,
        out_shape=[jax.ShapeDtypeStruct((rows // 2, width, 128), BF16)] * 4,
        grid=(rows // (2 * PAIRS),),
        in_specs=[
            whole_block(table.shape),
            pl.BlockSpec((8, 2 * PAIRS, orders, 128), lambda g: (0, g, 0, 0)),
        ],
        out_specs=[pl.BlockSpec((PAIRS, width, 128), lambda g: (g, 0, 0))] * 4,
        compiler_params=params(),
        cost_estimate=cost(rows * 64 * 4 * width * 16 * orders * 2, rows * 64 * 4 * width * 4),
        name="inverse_rows",
    )(table, data)


def join_kernel(place, *refs):
    data, out = refs[:4], refs[-1]
    for here in range(4):

        @pl.when(place[0] == here)
        def _():
            blocks = [data[here ^ j][0] for j in range(4)]
            for r in range(2):
                out[r] = jnp.concatenate(
                    [block[:, 64 * r : 64 * r + 64] for block in blocks], axis=1
                )


def join_part(part, place, data, prior):
    pairs, width, _ = data[0].shape
    first = prior is None
    return pl.pallas_call(
        join_kernel,
        out_shape=jax.ShapeDtypeStruct((2 * pairs * PARTS, width, 256), BF16),
        grid_spec=pltpu.PrefetchScalarGridSpec(
            num_scalar_prefetch=1,
            grid=(pairs,),
            in_specs=[pl.BlockSpec((1, width, 128), lambda g, _: (g, 0, 0))] * 4
            + ([] if first else [pl.BlockSpec(memory_space=pl.ANY)]),
            out_specs=pl.BlockSpec((2, width, 256), lambda g, _: (part * pairs + g, 0, 0)),
        ),
        input_output_aliases={} if first else {5: 0},
        compiler_params=params(),
        cost_estimate=cost(0, pairs * width * 256 * 8),
        name="join_rows",
    )(place, *data, *(() if first else (prior,)))


def exchange(pieces, axis):
    count = lax.axis_size(axis)
    return [pieces[0]] + [
        lax.ppermute(pieces[s], axis, [(i, i ^ s) for i in range(count)])
        for s in range(1, count)
    ]


def swap(values, axis):
    return lax.all_to_all(values, axis, split_axis=0, concat_axis=0, tiled=True)


def fourier_pair(blocks):
    orders = jnp.arange(L, dtype=jnp.int32)
    width = NLON // blocks.shape[0]
    longitude = blocks[:, None, None] * width + jnp.arange(width, dtype=jnp.int32)
    phase = (longitude * orders[None, :, None]) % NLON
    angle = phase.astype(F32) * (2.0 * math.pi / NLON)
    forward = jnp.concatenate([jnp.cos(angle), -jnp.sin(angle)], axis=1).astype(BF16)
    factor = jnp.where(orders == 0, 1.0, 2.0).astype(BF16)
    inverse = forward * jnp.tile(factor, 2)[None, :, None]
    return forward, jnp.swapaxes(inverse, 1, 2)


def packed_shards(cube_cells, block_source, block_weight, lift_in, lift_out, spectral):
    lat_count = lax.axis_size("lat")
    lon_count = lax.axis_size("lon")
    lon_index = lax.axis_index("lon")
    rows = block_weight.shape[0]
    pairs = rows // (2 * PARTS)
    per_band = L // lat_count
    rim_tiles = SRC_DEV // 2
    own_orders = lax.axis_index("lat") * per_band + jnp.arange(per_band, dtype=jnp.int32)

    widened = extended(cube_cells, (("lon", 0),), rim_tiles)
    picks = (block_source[:, 0, :] - lon_index * SRC_DEV + rim_tiles) % (lon_count * SRC_DEV)
    picks = picks.reshape(-1)
    weight = block_weight[:, 0]
    blocks = lon_index ^ jnp.arange(lon_count, dtype=jnp.int32)
    forward, inverse = fourier_pair(blocks)
    lift_out = lift_out.reshape(-1, lon_count, 64)[:, blocks].reshape(lift_out.shape)
    place = lon_index.astype(jnp.int32).reshape(1)
    row_order = jnp.arange(NLAT, dtype=jnp.int32).reshape(lat_count, PARTS, 2 * pairs)
    row_order = jnp.swapaxes(row_order, 0, 1).reshape(NLAT)
    table, quadrature = legendre_table(own_orders, row_order)
    own_scale = lax.dynamic_slice_in_dim(quadrature, lax.axis_index("lat") * rows, rows)
    own_scale = jnp.repeat(own_scale, 64).reshape(PARTS, pairs // PAIRS, 1, 128 * PAIRS)

    pieces = []
    lifted = lift_part(0, pairs, picks, widened, weight, lift_in, lift_out)
    for part in range(PARTS):
        arrived = exchange(lifted, "lon")
        if part + 1 < PARTS:
            lifted = lift_part(part + 1, pairs, picks, widened, weight, lift_in, lift_out)
            arrived, lifted = lax.optimization_barrier((arrived, lifted))
        spectra = dft_part(forward, arrived, own_scale[part])
        gathered = swap(spectra, "lat").reshape(NLAT // PARTS, per_band, 128)
        pieces.append(jnp.swapaxes(gathered, 0, 1))
    analysis = analysis_all(table, pieces)
    split = analysis.reshape(per_band, lon_count, L // lon_count, 128)
    by_degree = swap(jnp.transpose(split, (1, 2, 0, 3)), "lon")
    returned = swap(mix_all(by_degree, spectral), "lon").reshape(L, per_band, 128)
    synthesized = synthesis_all(table, jnp.swapaxes(returned, 0, 1))
    grid_field = None
    ready = []
    for part in range(PARTS):
        sent = jnp.swapaxes(synthesized[part], 0, 1)
        sent = sent.reshape(lat_count, 2 * pairs, per_band, 128)
        if part >= 2:
            sent, _ = lax.optimization_barrier((sent, ready[part - 2]))
        placed = inverse_part(inverse, swap(sent, "lat"))
        ready.append(placed)
        grid_field = join_part(part, place, exchange(placed, "lon"), grid_field)
    return grid_field


def solution(mesh):
    packed = mesh.shape["lat"] == 8 and mesh.shape["lon"] == 4
    in_specs = (
        P(("lat", "lon"), None, None),
        P("lat", "lon", None),
        P("lat", "lon", None, None, None),
        P(),
        P(),
        P("lon", None, None),
    )
    out_specs = P("lat", "lon", None)
    return jax.shard_map(packed_shards if packed else shards, mesh=mesh, in_specs=in_specs, out_specs=out_specs, check_vma=False)
```
